32 devices in a mesh: layer: 4 (over x, core), row: 8 (over z, y).
Axes of the slice: x: 2, y: 2, z: 4, core: 2. Of those that a mesh axis runs over, the one named last changes fastest.
Arguments:
- conc: float32 [2, 128, 256, 512], P(None, 'layer', 'row'), may hold values from -10 to 10
- explicit_rate: bfloat16 [2, 128, 256, 512], P(None, 'layer', 'row'), may hold values from 0.029907227 to 0.23925781
- x_coef: bfloat16 [2, 128, 256, 512], P(None, 'layer', 'row'), may hold values from 4 to 400
- y_coef: bfloat16 [2, 128, 256, 512], P(None, 'layer', 'row'), may hold values from 300 to 5984
- z_inverse: bfloat16 [16, 128, 256, 512], P(None, 'layer', 'row'), may hold values from 0.13964844 to 0.6015625
- z_link: float32 [2, 8, 256, 512], P(None, 'layer', 'row'), may hold values from 0.5 to 1
Outputs:
- new_conc: float32 [2, 128, 256, 512], P(None, 'layer', 'row')
The draws below stay inside these ranges and needn't reach their ends.
All inputs are finite; a program needn't handle non-finite values.
Results may differ from the reference program's by a relative error of at most 0.0003.
Values sent between devices are 32-bit elements; how exact they have to be, the bound alone decides.
A program may use at most 384 MiB of HBM per device.

```python
import math
import jax
import jax.numpy as jnp
from jax import lax

NX = 512
NY = 256
NZ = 128
ZB = 16
SPECIES = 2
NCH = 8


def draw_z_inverse(key, part):
    spread = jax.random.uniform(key, (ZB, NZ, NY, NX), jnp.float32)
    level = 0.4 + 0.6 * spread
    column = lax.broadcasted_iota(jnp.int32, (ZB, 1, 1, 1), 0)
    layer_row = lax.broadcasted_iota(jnp.int32, (1, NZ, 1, 1), 1) % ZB
    same = (column == layer_row).astype(jnp.float32)
    return (0.35 * level + 0.25 * same).astype(jnp.bfloat16)


def steps_of(rng, shape, cuts, least, high):
    factor_of, own = 1.0, jax.random.fold_in(rng, 6)
    for position, shards_of in cuts:
        draws = jnp.exp(jax.random.uniform(jax.random.fold_in(own, position), (shards_of,), jnp.float32, least / len(cuts), high / len(cuts)))
        factor_of = factor_of * jnp.repeat(draws, shape[position] // shards_of).reshape([-1 if axis == position else 1 for axis in range(len(shape))])
    return factor_of


def normal_values(key, extent, scale, bound, pieces=(), kind=jnp.bfloat16):
    values = scale * jax.random.normal(key, extent, jnp.float32)
    if pieces:
        values = values * steps_of(key, extent, pieces, -0.22, 0.18)
    return jnp.clip(values, -bound, bound).astype(kind)


def setup_inputs(seed: int = 0) -> dict:
    arg_keys = jax.random.split(jax.random.key(seed), 7)
    return {
        "conc": normal_values(arg_keys[0], (SPECIES, NZ, NY, NX), 2.0, 10.0, ((1, 4), (2, 8)), jnp.float32),
        "explicit_rate": jnp.clip(jnp.exp(math.log(0.23925781) - 2.0794415 * jax.random.uniform(arg_keys[1], (2, NZ, NY, NX), jnp.float32) ** steps_of(arg_keys[1], (2, NZ, NY, NX), ((1, 4), (2, 8)), -0.2, 0.2)), 0.029907227, 0.23925781).astype(jnp.bfloat16),
        "x_coef": jnp.clip(jnp.exp(math.log(400.0) - 4.6051702 * jax.random.uniform(arg_keys[2], (2, NZ, NY, NX), jnp.float32) ** steps_of(arg_keys[2], (2, NZ, NY, NX), ((1, 4), (2, 8)), -0.2, 0.2)), 4.0, 400.0).astype(jnp.bfloat16),
        "y_coef": jnp.clip(jnp.exp(math.log(5984.0) - 2.993062 * jax.random.uniform(arg_keys[3], (2, NZ, NY, NX), jnp.float32) ** steps_of(arg_keys[3], (2, NZ, NY, NX), ((1, 4), (2, 8)), -0.2, 0.2)), 300.0, 5984.0).astype(jnp.bfloat16),
        "z_inverse": draw_z_inverse(jax.random.fold_in(arg_keys[6], 71), 0),
        "z_link": jnp.clip(jnp.exp(math.log(1.0) - 0.6931472 * jax.random.uniform(arg_keys[5], (2, NCH, NY, NX), jnp.float32) ** steps_of(arg_keys[5], (2, NCH, NY, NX), ((1, 4), (2, 8)), -0.2, 0.2)), 0.5, 1.0),
    }


def shifted(values, stride, line_axis, forward):
    line_axis = line_axis % values.ndim
    length = values.shape[line_axis]
    if stride >= length:
        return jnp.zeros_like(values)
    widths = [(0, 0)] * values.ndim
    if forward:
        retained = lax.slice_in_dim(values, 0, length - stride, axis=line_axis)
        widths[line_axis] = (stride, 0)
    else:
        retained = lax.slice_in_dim(values, stride, length, axis=line_axis)
        widths[line_axis] = (0, stride)
    return jnp.pad(retained, widths)


def cyclic_reduce(lower_band, upper_band, right_side, line_axis):
    length = lower_band.shape[line_axis % lower_band.ndim]
    stride = 1
    while stride < length:
        lower_before = shifted(lower_band, stride, line_axis, True)
        upper_before = shifted(upper_band, stride, line_axis, True)
        lower_after = shifted(lower_band, stride, line_axis, False)
        upper_after = shifted(upper_band, stride, line_axis, False)
        right_before = shifted(right_side, stride, line_axis, True)
        right_after = shifted(right_side, stride, line_axis, False)
        factor = 1.0 / (1.0 - lower_band * upper_before - upper_band * lower_after)
        right_side = (right_side + lower_band * right_before + upper_band * right_after) * factor
        lower_band, upper_band = lower_band * lower_before * factor, upper_band * upper_after * factor
        stride = stride * 2
    return right_side


def normalized(coefficient, values):
    toward_low = coefficient[0].astype(jnp.float32)
    toward_high = coefficient[1].astype(jnp.float32)
    inverse_diag = 1.0 / (1.0 + toward_low + toward_high)
    return toward_low * inverse_diag, toward_high * inverse_diag, values * inverse_diag


def interface_solve(top_value, bottom_value, top_low, bottom_low, top_high, bottom_high):
    def forward(state_pair, entries):
        offset_part, slope_part = state_pair
        head_value, tail_value, head_low, tail_low, head_high, tail_high = entries
        factor = 1.0 / (1.0 - head_low * slope_part)
        base_part = (head_value + head_low * offset_part) * factor
        gain_part = head_high * factor
        next_offset = tail_value + tail_low * offset_part + tail_low * slope_part * base_part
        next_slope = tail_high + tail_low * slope_part * gain_part
        return (next_offset, next_slope), (base_part, gain_part, offset_part, slope_part)

    initial = (jnp.zeros_like(top_value[0]), jnp.zeros_like(top_low[0]))
    _, stored = lax.scan(forward, initial, (top_value, bottom_value, top_low, bottom_low, top_high, bottom_high))

    def backward(top_later, entries):
        base_part, gain_part, offset_part, slope_part = entries
        top_here = base_part + gain_part * top_later
        bottom_before = offset_part + slope_part * top_here
        return top_here, (bottom_before, top_later)

    _, (bottom_before, top_after) = lax.scan(backward, jnp.zeros_like(top_value[0]), stored, reverse=True)
    return bottom_before, top_after


def vertical_pieces(values, inverse, link):
    block_size = inverse.shape[0]
    block_count = values.shape[1] // block_size
    grouped = values.reshape(values.shape[0], block_count, block_size, values.shape[2], values.shape[3])
    inverse_blocks = inverse.reshape(block_size, block_count, block_size, inverse.shape[2], inverse.shape[3])
    local_part = None
    for column in range(block_size):
        product_term = inverse_blocks[column].astype(jnp.float32)[None] * grouped[:, :, column:column + 1]
        local_part = product_term if column == 0 else local_part + product_term
    low_spike = link[0].astype(jnp.float32)[:, None] * inverse_blocks[0].astype(jnp.float32)
    high_spike = link[1].astype(jnp.float32)[:, None] * inverse_blocks[block_size - 1].astype(jnp.float32)
    return local_part, low_spike, high_spike


def reference(conc, explicit_rate, x_coef, y_coef, z_inverse, z_link):
    rate_pair = explicit_rate.astype(jnp.float32)
    padded = jnp.pad(conc, ((0, 0), (1, 1), (1, 1), (0, 0)))
    center = padded[:, 1:-1, 1:-1]
    across_rows = padded[:, 1:-1, :-2] + padded[:, 1:-1, 2:] - 2.0 * center
    across_layers = padded[:, :-2, 1:-1] + padded[:, 2:, 1:-1] - 2.0 * center
    explicit = center + rate_pair[0] * across_rows + rate_pair[1] * across_layers

    def horizontal(entries):
        layer_values, layer_xcoef, layer_ycoef = entries
        low_band, high_band, scaled = normalized(layer_xcoef, layer_values)
        first_pass = cyclic_reduce(low_band, high_band, scaled, -1)
        low_band, high_band, scaled = normalized(layer_ycoef, first_pass)
        return cyclic_reduce(low_band, high_band, scaled, -2)

    middle = lax.map(horizontal, (jnp.moveaxis(explicit, 1, 0), jnp.moveaxis(x_coef, 1, 0), jnp.moveaxis(y_coef, 1, 0)))
    middle = jnp.moveaxis(middle, 0, 1)
    local_part, low_spike, high_spike = vertical_pieces(middle, z_inverse, z_link)
    final_row = low_spike.shape[1] - 1
    bottom_before, top_after = interface_solve(
        jnp.moveaxis(local_part[:, :, 0], 1, 0), jnp.moveaxis(local_part[:, :, final_row], 1, 0),
        low_spike[:, 0], low_spike[:, final_row], high_spike[:, 0], high_spike[:, final_row])
    result = local_part + low_spike[None] * jnp.moveaxis(bottom_before, 0, 1)[:, :, None] \
        + high_spike[None] * jnp.moveaxis(top_after, 0, 1)[:, :, None]
    return result.reshape(conc.shape)
```

```python
import functools

import jax
import jax.numpy as jnp
from jax import lax
from jax.experimental import pallas as pl
from jax.experimental.pallas import tpu as pltpu
from jax.sharding import PartitionSpec as P

F32 = jnp.float32
LANES = 128
SUB = 8


def neighbours(shard, axis, dim):
    devices, length = lax.axis_size(axis), shard.shape[dim]
    up = [(i, i + 1) for i in range(devices - 1)]
    down = [(j, i) for i, j in up]
    last = lax.slice_in_dim(shard, length - 1, length, axis=dim)
    first = lax.slice_in_dim(shard, 0, 1, axis=dim)
    return lax.ppermute(last, axis, up), lax.ppermute(first, axis, down)


def horizontal_kernel(
    conc, zlo, zhi, ylo, yhi, rate, xc, yc,
    solved, low_out, high_out, ends,
    lo_s, hi_s, rhs, ya, yb,
):
    species, nz, ny, nx = conc.shape
    blocks = nx // LANES
    per = LANES // ny
    groups = nz // per
    row = lax.broadcasted_iota(jnp.int32, (ny, nx), 0)

    def explicit_of(s, z):
        here = conc[s, z]
        before = jnp.where(row == 0, ylo[s, z], pltpu.roll(here, 1, 0))
        after = jnp.where(row == ny - 1, yhi[s, z], pltpu.roll(here, ny - 1, 0))
        below = zlo[s, 0] if z == 0 else conc[s, z - 1]
        above = zhi[s, 0] if z == nz - 1 else conc[s, z + 1]
        r0 = rate[0, z].astype(F32)
        r1 = rate[1, z].astype(F32)
        two = 2.0 * here
        return here + r0 * (before + after - two) + r1 * (below + above - two)

    def put(ref, g, tall):
        for q in range(blocks):
            ref[pl.ds(q * LANES * SUB + g, LANES, stride=SUB), :] = tall[
                :, q * LANES : (q + 1) * LANES
            ].T

    for g in range(groups):
        zs = range(g * per, (g + 1) * per)
        for s in range(species):
            put(rhs.at[s], g, jnp.concatenate([explicit_of(s, z) for z in zs], 0))
        put(lo_s, g, jnp.concatenate([xc[0, z].astype(F32) for z in zs], 0))
        put(hi_s, g, jnp.concatenate([xc[1, z].astype(F32) for z in zs], 0))

    half = nx // 2
    zero = jnp.zeros((SUB, LANES), F32)
    one = jnp.ones((SUB, LANES), F32)

    def at(i):
        return pl.ds(pl.multiple_of(i * SUB, SUB), SUB)

    def forward(i, state):
        gl, gr, fl, fr, _, _ = state
        j = nx - 1 - i
        a, b = lo_s[at(i), :], hi_s[at(i), :]
        e = 1.0 + a * gl
        r = 1.0 / (e + b)
        cl = b * r
        gl = e * r
        fl = tuple((rhs[s, at(i), :] + a * fl[s]) * r for s in range(species))
        hi_s[at(i), :] = cl
        a, b = lo_s[at(j), :], hi_s[at(j), :]
        e = 1.0 + b * gr
        r = 1.0 / (e + a)
        cr = a * r
        gr = e * r
        fr = tuple((rhs[s, at(j), :] + b * fr[s]) * r for s in range(species))
        lo_s[at(j), :] = cr
        for s in range(species):
            rhs[s, at(i), :] = fl[s]
            rhs[s, at(j), :] = fr[s]
        return gl, gr, fl, fr, cl, cr

    start = (one, one, (zero,) * species, (zero,) * species, zero, zero)
    gl, gr, fl, fr, cl, cr = lax.fori_loop(0, half, forward, start, unroll=4)
    meet = 1.0 / (gl + cl * gr)
    ul = tuple((fl[s] + cl * fr[s]) * meet for s in range(species))
    ur = tuple((fr[s] + cr * fl[s]) * meet for s in range(species))
    for s in range(species):
        rhs[s, at(half - 1), :] = ul[s]
        rhs[s, at(half), :] = ur[s]

    def backward(t, state):
        ul, ur = state
        i = half - 2 - t
        j = half + 1 + t
        cl = hi_s[at(i), :]
        cr = lo_s[at(j), :]
        ul = tuple(rhs[s, at(i), :] + cl * ul[s] for s in range(species))
        ur = tuple(rhs[s, at(j), :] + cr * ur[s] for s in range(species))
        for s in range(species):
            rhs[s, at(i), :] = ul[s]
            rhs[s, at(j), :] = ur[s]
        return ul, ur

    lax.fori_loop(0, half - 1, backward, (ul, ur), unroll=5)

    for g in range(groups):
        for q in range(blocks):
            for s in range(species):
                wide = rhs[s, pl.ds(q * LANES * SUB + g, LANES, stride=SUB), :].T
                for p in range(per):
                    solved[s, q, pl.ds(g * per + p, ny, stride=nz), :] = wide[
                        p * ny : (p + 1) * ny
                    ]
    for z in range(nz):
        a, b = yc[0, z].astype(F32), yc[1, z].astype(F32)
        for q in range(blocks):
            cols = slice(q * LANES, (q + 1) * LANES)
            ya[q, pl.ds(z, ny, stride=nz), :] = a[:, cols]
            yb[q, pl.ds(z, ny, stride=nz), :] = b[:, cols]

    def line(q, _):
        tile = (nz, LANES)
        g = jnp.ones(tile, F32)
        f = [jnp.zeros(tile, F32) for _ in range(species)]
        spike = jnp.ones(tile, F32)
        for y in range(ny):
            rows = pl.ds(y * nz, nz)
            a, b = ya[q, rows, :], yb[q, rows, :]
            e = 1.0 + a * g
            r = 1.0 / (e + b)
            g = e * r
            ar = a * r
            c = b * r
            f = [solved[s, q, rows, :] * r + ar * f[s] for s in range(species)]
            spike = ar * spike
            for s in range(species):
                solved[s, q, rows, :] = f[s]
            low_out[q, rows, :] = spike
            high_out[q, rows, :] = c
        for s in range(species):
            ends[species + s, q] = f[s]
        ends[2 * species + 1, q] = spike
        ends[2 * species + 3, q] = c
        high = c
        low = spike
        for y in range(ny - 2, -1, -1):
            rows = pl.ds(y * nz, nz)
            c = high_out[q, rows, :]
            f = [solved[s, q, rows, :] + c * f[s] for s in range(species)]
            low = low_out[q, rows, :] + c * low
            high = c * high
            for s in range(species):
                solved[s, q, rows, :] = f[s]
            low_out[q, rows, :] = low
            high_out[q, rows, :] = high
        for s in range(species):
            ends[s, q] = f[s]
        ends[2 * species, q] = low
        ends[2 * species + 2, q] = high
        return 0

    lax.fori_loop(0, blocks, line, 0)


def horizontal(conc, rate, x_coef, y_coef):
    species, nz, ny, nx = conc.shape
    blocks = nx // LANES
    zlo, zhi = neighbours(conc, "layer", 1)
    ylo, yhi = neighbours(conc, "row", 2)
    flat = (blocks, ny * nz, LANES)
    shape = lambda *dims: jax.ShapeDtypeStruct(dims, F32)
    vmem = pl.BlockSpec(memory_space=pltpu.VMEM)
    return pl.pallas_call(
        horizontal_kernel,
        out_shape=(
            shape(species, *flat),
            shape(*flat),
            shape(*flat),
            shape(2 * species + 4, blocks, nz, LANES),
        ),
        in_specs=[vmem] * 8,
        out_specs=(vmem,) * 4,
        scratch_shapes=[
            pltpu.VMEM((nx * SUB, LANES), F32),
            pltpu.VMEM((nx * SUB, LANES), F32),
            pltpu.VMEM((species, nx * SUB, LANES), F32),
            pltpu.VMEM(flat, F32),
            pltpu.VMEM(flat, F32),
        ],
        compiler_params=pltpu.CompilerParams(vmem_limit_bytes=50 * 1024 * 1024),
        name="horizontal",
    )(conc, zlo, zhi, ylo, yhi, rate, x_coef, y_coef)


def vertical_kernel(solved, low, high, before, after, inverse, link, part, ends, mid):
    species, width = solved.shape[0], solved.shape[1]
    ny = solved.shape[2]
    size = inverse.shape[0]
    for q in range(width):
        for y in range(ny):
            lo, hi = low[q, y], high[q, y]
            for s in range(species):
                value = solved[s, q, y] + lo * before[s, q] + hi * after[s, q]
                mid[s, q, pl.ds(y, size, stride=ny), :] = value

    for q in range(width):
        cols = slice(q * LANES, (q + 1) * LANES)

        def layer(z, _):
            total = [None] * species
            for j in range(size):
                v = inverse[j, z, :, cols].astype(F32)
                for s in range(species):
                    term = v * mid[s, q, j * ny : (j + 1) * ny, :]
                    total[s] = term if j == 0 else total[s] + term
            for s in range(species):
                part[s, z, :, cols] = total[s]
            return 0

        lax.fori_loop(0, size, layer, 0)
        l0, l1 = link[0, 0, :, cols], link[1, 0, :, cols]
        for e, z in enumerate((0, size - 1)):
            for s in range(species):
                ends[0, e * species + s, :, cols] = part[s, z, :, cols]
            ends[0, 2 * species + e, :, cols] = l0 * inverse[0, z, :, cols].astype(F32)
            ends[0, 2 * species + 2 + e, :, cols] = l1 * inverse[size - 1, z, :, cols].astype(F32)


def vertical(solved, low, high, before, after, inverse, link):
    species, blocks = solved.shape[:2]
    size, nz, ny, nx = inverse.shape
    count = nz // size
    tile = 16
    width = 2
    wide = width * LANES
    solved = solved.reshape(species, blocks, ny, nz, LANES)
    low = low.reshape(blocks, ny, nz, LANES)
    high = high.reshape(blocks, ny, nz, LANES)
    values = 2 * species + 4
    part_spec = pl.BlockSpec((species, size, tile, wide), lambda k, y, q: (0, k, y, q))
    side_spec = pl.BlockSpec((species, width, size, LANES), lambda k, y, q: (0, q, k, 0))
    spike_spec = pl.BlockSpec((width, tile, size, LANES), lambda k, y, q: (q, y, k, 0))
    return pl.pallas_call(
        vertical_kernel,
        grid=(count, ny // tile, blocks // width),
        out_shape=(
            jax.ShapeDtypeStruct((species, nz, ny, nx), F32),
            jax.ShapeDtypeStruct((count, values, ny, nx), F32),
        ),
        in_specs=[
            pl.BlockSpec((species, width, tile, size, LANES), lambda k, y, q: (0, q, y, k, 0)),
            spike_spec,
            spike_spec,
            side_spec,
            side_spec,
            pl.BlockSpec((size, size, tile, wide), lambda k, y, q: (0, k, y, q)),
            pl.BlockSpec((2, 1, tile, wide), lambda k, y, q: (0, k, y, q)),
        ],
        out_specs=(
            part_spec,
            pl.BlockSpec((1, values, tile, wide), lambda k, y, q: (k, 0, y, q)),
        ),
        scratch_shapes=[pltpu.VMEM((species, width, size * tile, LANES), F32)],
        compiler_params=pltpu.CompilerParams(vmem_limit_bytes=40 * 1024 * 1024),
        name="vertical",
    )(solved, low, high, before, after, inverse, link)


def chain(entries, species):
    offset = jnp.zeros_like(entries[0][:species])
    slope = jnp.zeros_like(entries[0][0])
    stored = []
    for item in entries:
        head, tail = item[:species], item[species : 2 * species]
        head_low, tail_low, head_high, tail_high = (item[2 * species + i] for i in range(4))
        factor = 1.0 / (1.0 - head_low * slope)
        base = (head + head_low * offset) * factor
        gain = head_high * factor
        stored.append((base, gain, offset, slope))
        offset = tail + tail_low * offset + tail_low * slope * base
        slope = tail_high + tail_low * slope * gain
    later = jnp.zeros_like(offset)
    results = []
    for base, gain, offset, slope in reversed(stored):
        here = base + gain * later
        results.append(jnp.concatenate([offset + slope * here, later], 0))
        later = here
    return results[::-1]


def local(conc, explicit_rate, x_coef, y_coef, z_inverse, z_link):
    species, nz, ny, nx = conc.shape
    values = 2 * species + 4
    solved, low, high, ends = horizontal(conc, explicit_rate, x_coef, y_coef)
    rows = lax.axis_size("row")
    blocks = ends.shape[1]
    cut = ends.reshape(values, blocks, rows, nz // rows, LANES)
    cut = jnp.moveaxis(cut, 2, 0)
    cut = lax.all_to_all(cut, "row", 0, 0)
    answer = jnp.stack(chain([cut[i] for i in range(rows)], species), 0)
    answer = lax.all_to_all(answer, "row", 0, 0)
    answer = jnp.moveaxis(answer, 0, 2).reshape(2 * species, blocks, nz, LANES)
    part, ends = vertical(
        solved, low, high, answer[:species], answer[species:], z_inverse, z_link
    )
    layers = lax.axis_size("layer")
    count = ends.shape[0]
    cut = ends.reshape(count, values, layers, ny // layers, nx)
    cut = jnp.moveaxis(cut, 2, 0)
    cut = lax.all_to_all(cut, "layer", 0, 0)
    answer = chain([cut[i, k] for i in range(layers) for k in range(count)], species)
    answer = jnp.stack(answer, 0).reshape(layers, count, 2 * species, ny // layers, nx)
    answer = lax.all_to_all(answer, "layer", 0, 0)
    answer = jnp.moveaxis(answer, 0, 2).reshape(count, 2 * species, ny, nx)
    size = z_inverse.shape[0]
    out = part.reshape(species, count, size, ny, nx)
    first = z_inverse[0].reshape(count, size, ny, nx).astype(F32)
    last = z_inverse[size - 1].reshape(count, size, ny, nx).astype(F32)
    below = jnp.moveaxis(answer[:, :species], 1, 0) * z_link[0][None]
    above = jnp.moveaxis(answer[:, species:], 1, 0) * z_link[1][None]
    out = out + first[None] * below[:, :, None] + last[None] * above[:, :, None]
    return out.reshape(conc.shape)


def solution(mesh):
    placed = P(None, "layer", "row", None)
    return jax.shard_map(
        local, mesh=mesh, in_specs=(placed,) * 6, out_specs=placed, check_vma=False
    )
```

```python
import functools

import jax
import jax.numpy as jnp
from jax import lax
from jax.experimental import pallas as pl
from jax.experimental.pallas import tpu as pltpu
from jax.sharding import PartitionSpec as P

F32 = jnp.float32
LANES = 128
SUB = 8


def neighbours(shard, axis, dim):
    devices, length = lax.axis_size(axis), shard.shape[dim]
    up = [(i, i + 1) for i in range(devices - 1)]
    down = [(j, i) for i, j in up]
    last = lax.slice_in_dim(shard, length - 1, length, axis=dim)
    first = lax.slice_in_dim(shard, 0, 1, axis=dim)
    return lax.ppermute(last, axis, up), lax.ppermute(first, axis, down)


def horizontal_kernel(
    conc, zlo, zhi, ylo, yhi, rate, xc, yc,
    solved, low_out, high_out, ends,
    lo_s, hi_s, rhs, ya, yb,
):
    species, nz, ny, nx = conc.shape
    blocks = nx // LANES
    per = LANES // ny
    groups = nz // per
    row = lax.broadcasted_iota(jnp.int32, (ny, nx), 0)

    def explicit_of(s, z):
        here = conc[s, z]
        before = jnp.where(row == 0, ylo[s, z], pltpu.roll(here, 1, 0))
        after = jnp.where(row == ny - 1, yhi[s, z], pltpu.roll(here, ny - 1, 0))
        below = zlo[s, 0] if z == 0 else conc[s, z - 1]
        above = zhi[s, 0] if z == nz - 1 else conc[s, z + 1]
        r0 = rate[0, z].astype(F32)
        r1 = rate[1, z].astype(F32)
        two = 2.0 * here
        return here + r0 * (before + after - two) + r1 * (below + above - two)

    def put(ref, g, tall):
        for q in range(blocks):
            ref[pl.ds(q * LANES * SUB + g, LANES, stride=SUB), :] = tall[
                :, q * LANES : (q + 1) * LANES
            ].T

    for g in range(groups):
        zs = range(g * per, (g + 1) * per)
        for s in range(species):
            put(rhs.at[s], g, jnp.concatenate([explicit_of(s, z) for z in zs], 0))
        put(lo_s, g, jnp.concatenate([xc[0, z].astype(F32) for z in zs], 0))
        put(hi_s, g, jnp.concatenate([xc[1, z].astype(F32) for z in zs], 0))

    half = nx // 2
    zero = jnp.zeros((SUB, LANES), F32)
    one = jnp.ones((SUB, LANES), F32)

    def at(i):
        return pl.ds(pl.multiple_of(i * SUB, SUB), SUB)

    def forward(i, state):
        gl, gr, fl, fr, _, _ = state
        j = nx - 1 - i
        a, b = lo_s[at(i), :], hi_s[at(i), :]
        e = 1.0 + a * gl
        r = 1.0 / (e + b)
        cl = b * r
        gl = e * r
        fl = tuple((rhs[s, at(i), :] + a * fl[s]) * r for s in range(species))
        hi_s[at(i), :] = cl
        a, b = lo_s[at(j), :], hi_s[at(j), :]
        e = 1.0 + b * gr
        r = 1.0 / (e + a)
        cr = a * r
        gr = e * r
        fr = tuple((rhs[s, at(j), :] + b * fr[s]) * r for s in range(species))
        lo_s[at(j), :] = cr
        for s in range(species):
            rhs[s, at(i), :] = fl[s]
            rhs[s, at(j), :] = fr[s]
        return gl, gr, fl, fr, cl, cr

    start = (one, one, (zero,) * species, (zero,) * species, zero, zero)
    gl, gr, fl, fr, cl, cr = lax.fori_loop(0, half, forward, start, unroll=4)
    meet = 1.0 / (gl + cl * gr)
    ul = tuple((fl[s] + cl * fr[s]) * meet for s in range(species))
    ur = tuple((fr[s] + cr * fl[s]) * meet for s in range(species))
    for s in range(species):
        rhs[s, at(half - 1), :] = ul[s]
        rhs[s, at(half), :] = ur[s]

    def backward(t, state):
        ul, ur = state
        i = half - 2 - t
        j = half + 1 + t
        cl = hi_s[at(i), :]
        cr = lo_s[at(j), :]
        ul = tuple(rhs[s, at(i), :] + cl * ul[s] for s in range(species))
        ur = tuple(rhs[s, at(j), :] + cr * ur[s] for s in range(species))
        for s in range(species):
            rhs[s, at(i), :] = ul[s]
            rhs[s, at(j), :] = ur[s]
        return ul, ur

    lax.fori_loop(0, half - 1, backward, (ul, ur), unroll=5)

    for g in range(groups):
        for q in range(blocks):
            for s in range(species):
                wide = rhs[s, pl.ds(q * LANES * SUB + g, LANES, stride=SUB), :].T
                for p in range(per):
                    solved[s, q, pl.ds(g * per + p, ny, stride=nz), :] = wide[
                        p * ny : (p + 1) * ny
                    ]
    for z in range(nz):
        a, b = yc[0, z].astype(F32), yc[1, z].astype(F32)
        for q in range(blocks):
            cols = slice(q * LANES, (q + 1) * LANES)
            ya[q, pl.ds(z, ny, stride=nz), :] = a[:, cols]
            yb[q, pl.ds(z, ny, stride=nz), :] = b[:, cols]

    def line(q, _):
        tile = (nz, LANES)
        g = jnp.ones(tile, F32)
        f = [jnp.zeros(tile, F32) for _ in range(species)]
        spike = jnp.ones(tile, F32)
        for y in range(ny):
            rows = pl.ds(y * nz, nz)
            a, b = ya[q, rows, :], yb[q, rows, :]
            e = 1.0 + a * g
            r = 1.0 / (e + b)
            g = e * r
            ar = a * r
            c = b * r
            f = [solved[s, q, rows, :] * r + ar * f[s] for s in range(species)]
            spike = ar * spike
            for s in range(species):
                solved[s, q, rows, :] = f[s]
            low_out[q, rows, :] = spike
            high_out[q, rows, :] = c
        for s in range(species):
            ends[species + s, q] = f[s]
        ends[2 * species + 1, q] = spike
        ends[2 * species + 3, q] = c
        high = c
        low = spike
        for y in range(ny - 2, -1, -1):
            rows = pl.ds(y * nz, nz)
            c = high_out[q, rows, :]
            f = [solved[s, q, rows, :] + c * f[s] for s in range(species)]
            low = low_out[q, rows, :] + c * low
            high = c * high
            for s in range(species):
                solved[s, q, rows, :] = f[s]
            low_out[q, rows, :] = low
            high_out[q, rows, :] = high
        for s in range(species):
            ends[s, q] = f[s]
        ends[2 * species, q] = low
        ends[2 * species + 2, q] = high
        return 0

    lax.fori_loop(0, blocks, line, 0)


def horizontal(conc, rate, x_coef, y_coef):
    species, nz, ny, nx = conc.shape
    blocks = nx // LANES
    zlo, zhi = neighbours(conc, "layer", 1)
    ylo, yhi = neighbours(conc, "row", 2)
    flat = (blocks, ny * nz, LANES)
    shape = lambda *dims: jax.ShapeDtypeStruct(dims, F32)
    vmem = pl.BlockSpec(memory_space=pltpu.VMEM)
    return pl.pallas_call(
        horizontal_kernel,
        out_shape=(
            shape(species, *flat),
            shape(*flat),
            shape(*flat),
            shape(2 * species + 4, blocks, nz, LANES),
        ),
        in_specs=[vmem] * 8,
        out_specs=(vmem,) * 4,
        scratch_shapes=[
            pltpu.VMEM((nx * SUB, LANES), F32),
            pltpu.VMEM((nx * SUB, LANES), F32),
            pltpu.VMEM((species, nx * SUB, LANES), F32),
            pltpu.VMEM(flat, F32),
            pltpu.VMEM(flat, F32),
        ],
        compiler_params=pltpu.CompilerParams(vmem_limit_bytes=50 * 1024 * 1024),
        name="horizontal",
    )(conc, zlo, zhi, ylo, yhi, rate, x_coef, y_coef)


def vertical_kernel(solved, low, high, before, after, inverse, link, part, ends, mid):
    species, width = solved.shape[0], solved.shape[1]
    ny = solved.shape[2]
    size = inverse.shape[0]
    for q in range(width):
        for y in range(ny):
            lo, hi = low[q, y], high[q, y]
            for s in range(species):
                value = solved[s, q, y] + lo * before[s, q] + hi * after[s, q]
                mid[s, q, pl.ds(y, size, stride=ny), :] = value

    for q in range(width):
        cols = slice(q * LANES, (q + 1) * LANES)

        def layer(z, _):
            total = [None] * species
            for j in range(size):
                v = inverse[j, z, :, cols].astype(F32)
                for s in range(species):
                    term = v * mid[s, q, j * ny : (j + 1) * ny, :]
                    total[s] = term if j == 0 else total[s] + term
            for s in range(species):
                part[s, z, :, cols] = total[s]
            return 0

        lax.fori_loop(0, size, layer, 0)
        l0, l1 = link[0, 0, :, cols], link[1, 0, :, cols]
        for e, z in enumerate((0, size - 1)):
            for s in range(species):
                ends[0, e * species + s, :, cols] = part[s, z, :, cols]
            ends[0, 2 * species + e, :, cols] = l0 * inverse[0, z, :, cols].astype(F32)
            ends[0, 2 * species + 2 + e, :, cols] = l1 * inverse[size - 1, z, :, cols].astype(F32)


def vertical(solved, low, high, before, after, inverse, link):
    species, blocks = solved.shape[:2]
    size, nz, ny, nx = inverse.shape
    count = nz // size
    tile = 16
    width = 2
    wide = width * LANES
    solved = solved.reshape(species, blocks, ny, nz, LANES)
    low = low.reshape(blocks, ny, nz, LANES)
    high = high.reshape(blocks, ny, nz, LANES)
    values = 2 * species + 4
    part_spec = pl.BlockSpec((species, size, tile, wide), lambda k, y, q: (0, k, y, q))
    side_spec = pl.BlockSpec((species, width, size, LANES), lambda k, y, q: (0, q, k, 0))
    spike_spec = pl.BlockSpec((width, tile, size, LANES), lambda k, y, q: (q, y, k, 0))
    return pl.pallas_call(
        vertical_kernel,
        grid=(count, ny // tile, blocks // width),
        out_shape=(
            jax.ShapeDtypeStruct((species, nz, ny, nx), F32),
            jax.ShapeDtypeStruct((count, values, ny, nx), F32),
        ),
        in_specs=[
            pl.BlockSpec((species, width, tile, size, LANES), lambda k, y, q: (0, q, y, k, 0)),
            spike_spec,
            spike_spec,
            side_spec,
            side_spec,
            pl.BlockSpec((size, size, tile, wide), lambda k, y, q: (0, k, y, q)),
            pl.BlockSpec((2, 1, tile, wide), lambda k, y, q: (0, k, y, q)),
        ],
        out_specs=(
            part_spec,
            pl.BlockSpec((1, values, tile, wide), lambda k, y, q: (k, 0, y, q)),
        ),
        scratch_shapes=[pltpu.VMEM((species, width, size * tile, LANES), F32)],
        compiler_params=pltpu.CompilerParams(vmem_limit_bytes=40 * 1024 * 1024),
        name="vertical",
    )(solved, low, high, before, after, inverse, link)


def chain(entries, species):
    offset = jnp.zeros_like(entries[0][:species])
    slope = jnp.zeros_like(entries[0][0])
    stored = []
    for item in entries:
        head, tail = item[:species], item[species : 2 * species]
        head_low, tail_low, head_high, tail_high = (item[2 * species + i] for i in range(4))
        factor = 1.0 / (1.0 - head_low * slope)
        base = (head + head_low * offset) * factor
        gain = head_high * factor
        stored.append((base, gain, offset, slope))
        offset = tail + tail_low * offset + tail_low * slope * base
        slope = tail_high + tail_low * slope * gain
    later = jnp.zeros_like(offset)
    results = []
    for base, gain, offset, slope in reversed(stored):
        here = base + gain * later
        results.append(jnp.concatenate([offset + slope * here, later], 0))
        later = here
    return results[::-1]


def exchange_kernel(axis, species, count, cut, final, inbox, answer, send, recv, send_back, recv_back):
    parts, _, rows, wide = cut.shape
    values = 2 * species + 4
    me = lax.axis_index(axis)
    mesh_id = pl.DeviceIdType.MESH
    peers = [lax.rem(me + d, parts) for d in range(1, parts)]
    barrier = pltpu.get_barrier_semaphore()
    for peer in peers:
        pl.semaphore_signal(barrier, inc=1, device_id={axis: peer}, device_id_type=mesh_id)
    pl.semaphore_wait(barrier, parts - 1)

    def copies(source, target, out_sem, in_sem):
        made = [
            pltpu.make_async_remote_copy(
                src_ref=source.at[peer],
                dst_ref=target.at[me],
                send_sem=out_sem.at[d],
                recv_sem=in_sem.at[d],
                device_id={axis: peer},
                device_id_type=mesh_id,
            )
            for d, peer in enumerate(peers)
        ]
        for copy in made:
            copy.start()
        return made

    there = copies(cut, inbox, send, recv)
    inbox[me] = cut[me]
    for copy in there:
        copy.wait_recv()
    step = min(rows, SUB)
    for t in range(rows // step):
        for c in range(wide // LANES):
            at = (slice(t * step, (t + 1) * step), slice(c * LANES, (c + 1) * LANES))
            entries = [
                inbox[i, k * values : (k + 1) * values, at[0], at[1]]
                for i in range(parts)
                for k in range(count)
            ]
            for n, result in enumerate(chain(entries, species)):
                i, k = divmod(n, count)
                answer[i, 2 * species * k : 2 * species * (k + 1), at[0], at[1]] = result
    back = copies(answer, final, send_back, recv_back)
    final[me] = answer[me]
    for copy in there:
        copy.wait_send()
    for copy in back:
        copy.wait()


def exchange(cut, axis, species, count, number):
    parts, _, rows, wide = cut.shape
    vmem = pl.BlockSpec(memory_space=pltpu.VMEM)
    reply = (parts, 2 * species * count, rows, wide)
    return pl.pallas_call(
        functools.partial(exchange_kernel, axis, species, count),
        out_shape=jax.ShapeDtypeStruct(reply, F32),
        in_specs=[vmem],
        out_specs=vmem,
        scratch_shapes=[pltpu.VMEM(cut.shape, F32), pltpu.VMEM(reply, F32)]
        + [pltpu.SemaphoreType.DMA((parts - 1,))] * 4,
        compiler_params=pltpu.CompilerParams(
            collective_id=number, has_side_effects=True, vmem_limit_bytes=24 * 1024 * 1024
        ),
        name="exchange_" + axis,
    )(cut)


def local(conc, explicit_rate, x_coef, y_coef, z_inverse, z_link):
    species, nz, ny, nx = conc.shape
    values = 2 * species + 4
    solved, low, high, ends = horizontal(conc, explicit_rate, x_coef, y_coef)
    rows = lax.axis_size("row")
    blocks = ends.shape[1]
    cut = ends.reshape(values, blocks, rows, nz // rows, LANES)
    cut = jnp.moveaxis(cut, 2, 0).reshape(rows, values, -1, LANES)
    answer = exchange(cut, "row", species, 1, 0)
    answer = answer.reshape(rows, 2 * species, blocks, nz // rows, LANES)
    answer = jnp.moveaxis(answer, 0, 2).reshape(2 * species, blocks, nz, LANES)
    part, ends = vertical(
        solved, low, high, answer[:species], answer[species:], z_inverse, z_link
    )
    layers = lax.axis_size("layer")
    count = ends.shape[0]
    cut = ends.reshape(count, values, layers, ny // layers, nx)
    cut = jnp.moveaxis(cut, 2, 0).reshape(layers, count * values, ny // layers, nx)
    answer = exchange(cut, "layer", species, count, 1)
    answer = answer.reshape(layers, count, 2 * species, ny // layers, nx)
    answer = jnp.moveaxis(answer, 0, 2).reshape(count, 2 * species, ny, nx)
    size = z_inverse.shape[0]
    out = part.reshape(species, count, size, ny, nx)
    first = z_inverse[0].reshape(count, size, ny, nx).astype(F32)
    last = z_inverse[size - 1].reshape(count, size, ny, nx).astype(F32)
    below = jnp.moveaxis(answer[:, :species], 1, 0) * z_link[0][None]
    above = jnp.moveaxis(answer[:, species:], 1, 0) * z_link[1][None]
    out = out + first[None] * below[:, :, None] + last[None] * above[:, :, None]
    return out.reshape(conc.shape)


def solution(mesh):
    placed = P(None, "layer", "row", None)
    return jax.shard_map(
        local, mesh=mesh, in_specs=(placed,) * 6, out_specs=placed, check_vma=False
    )
```
